32 devices in a mesh: node: 8 (over y, x, core), local: 4 (over z).
Axes of the slice: x: 2, y: 2, z: 4, core: 2. Of those that a mesh axis runs over, the one named last changes fastest.
Arguments:
- tokens: bfloat16 [1024, 7168], P('node', 'local'), may hold values from -6 to 6
- out_grad: bfloat16 [1024, 7168], P('node', 'local'), may hold values from -6 to 6
- expert_ids: int32 [1024, 8], P('node'), may hold values from 0 to 15, as said below
- gates: float32 [1024, 8], P('node'), may hold values from 0.05 to 1
- gate_weight: bfloat16 [16, 7168, 1024], P('node', 'local'), may hold values from -0.0625 to 0.0625
- up_weight: bfloat16 [16, 7168, 1024], P('node', 'local'), may hold values from -0.0625 to 0.0625
- down_weight: bfloat16 [16, 1024, 7168], P('node', None, 'local'), may hold values from -0.1875 to 0.1875
Outputs:
- grad_tokens: bfloat16 [1024, 7168], P('node', 'local')
- gate_grad: bfloat16 [16, 7168, 1024], P('node', 'local')
- up_grad: bfloat16 [16, 7168, 1024], P('node', 'local')
- down_grad: bfloat16 [16, 1024, 7168], P('node', None, 'local')
The draws below stay inside these ranges and needn't reach their ends.
Inputs may be any that keep to these rules, and one draw needn't show every extreme that they name: `expert_ids`: each row names 8 different experts, all within at most 4 routing groups, group g being experts g * 4 to g * 4 + 3.
All inputs are finite; a program needn't handle non-finite values.
Results may differ from the reference program's by a relative error of at most 0.029.
Values may be sent and summed in bfloat16 or wider, within the bound.
A program may use at most 128 MiB of HBM per device.

```python
import math
import jax
import jax.numpy as jnp
from jax import lax

D = 7168
F = 1024
TOP = 8
GROUP_EXP = 4
LIMIT = 4
TOK_NODE = 128
EXPERTS = 16
TOKENS = 1024
CAP = 80
N_NODE = 8
N_LOCAL = 4


def draw_expert_ids(key, part):
    key = jax.random.fold_in(key, 11)
    key_a, key_b, key_c, key_d = jax.random.split(key, 4)
    group_count = EXPERTS // GROUP_EXP
    group_bias = jax.random.randint(key_a, (group_count,), 0, 4) * 262144
    group_score = (jax.random.randint(key_b, (TOKENS, group_count), 0, 1048576) + group_bias[None, :]) * group_count
    group_score = group_score + jnp.arange(group_count, dtype=jnp.int32)[None, :]
    _, chosen = lax.top_k(group_score, LIMIT)
    allowed = jnp.any(chosen[:, :, None] == jnp.arange(group_count, dtype=jnp.int32)[None, None, :], axis=1)
    allowed_experts = jnp.repeat(allowed, GROUP_EXP, axis=1)
    expert_bias = jax.random.randint(key_c, (EXPERTS,), 0, 4) * 262144
    expert_score = (jax.random.randint(key_d, (TOKENS, EXPERTS), 0, 1048576) + expert_bias[None, :]) * EXPERTS
    expert_score = expert_score + jnp.arange(EXPERTS, dtype=jnp.int32)[None, :]
    expert_score = jnp.where(allowed_experts, expert_score, -1)
    _, picked = lax.top_k(expert_score, TOP)
    return picked.astype(jnp.int32)


def block_scale(rng, shape, pieces, low, high):
    gain = 1.0
    for axis_at, parts in pieces:
        steps = jax.random.uniform(jax.random.fold_in(jax.random.fold_in(rng, 6), axis_at), (parts,), jnp.float32, low / len(pieces), high / len(pieces))
        gain = gain * jnp.repeat(jnp.exp(steps), shape[axis_at] // parts).reshape((-1,) + (1,) * (len(shape) - 1 - axis_at))
    return gain


def gaussian(rng, dims, deviation, reach, pieces=(), held_as=jnp.bfloat16):
    level = block_scale(rng, dims, pieces, -0.22, 0.18) if pieces else 1.0
    result = jax.random.normal(rng, dims, jnp.float32) * deviation * level
    return jnp.minimum(jnp.maximum(result, -reach), reach).astype(held_as)


def setup_inputs(seed: int = 0) -> dict:
    key_of = jax.random.split(jax.random.key(seed), 8)
    return {
        "tokens": gaussian(key_of[0], (TOKENS, D), 1.0, 6.0, ((0, 8), (1, 4))),
        "out_grad": gaussian(key_of[1], (TOKENS, D), 1.0, 6.0, ((0, 8), (1, 4))),
        "expert_ids": draw_expert_ids(jax.random.fold_in(key_of[7], 71), 0),
        "gates": jnp.clip(jnp.exp(math.log(1.0) - 2.9957323 * jax.random.uniform(key_of[3], (TOKENS, TOP), jnp.float32) ** block_scale(key_of[3], (TOKENS, TOP), ((0, 8),), -0.2, 0.2)), 0.05, 1.0),
        "gate_weight": gaussian(key_of[4], (EXPERTS, D, F), D ** -0.5, 0.0625, ((0, 8), (1, 4))),
        "up_weight": gaussian(key_of[5], (EXPERTS, D, F), D ** -0.5, 0.0625, ((0, 8), (1, 4))),
        "down_weight": gaussian(key_of[6], (EXPERTS, F, D), F ** -0.5, 0.1875, ((0, 8), (2, 4))),
    }


def swiglu_backward(gate_pre, up_pre, grad_hidden):
    sigmoid_g = jax.nn.sigmoid(gate_pre)
    activated = gate_pre * sigmoid_g
    hidden_act = (activated * up_pre).astype(jnp.bfloat16)
    grad_gate = (grad_hidden * up_pre * sigmoid_g * (1.0 + gate_pre * (1.0 - sigmoid_g))).astype(jnp.bfloat16)
    grad_up = (grad_hidden * activated).astype(jnp.bfloat16)
    return hidden_act, grad_gate, grad_up


def rounded_term(value):
    return lax.optimization_barrier(value.astype(jnp.bfloat16)).astype(jnp.float32)


def expert_step(operands):
    x_rows, dy_rows, w_gate, w_up, w_down = operands
    width_slice = D // N_LOCAL
    gate_pre = jnp.zeros((x_rows.shape[0], F), jnp.float32)
    up_pre = jnp.zeros((x_rows.shape[0], F), jnp.float32)
    grad_hidden = jnp.zeros((x_rows.shape[0], F), jnp.float32)
    for piece in range(N_LOCAL):
        lower = piece * width_slice
        upper = lower + width_slice
        gate_pre = gate_pre + rounded_term(jnp.dot(x_rows[:, lower:upper], w_gate[lower:upper], preferred_element_type=jnp.float32))
        up_pre = up_pre + rounded_term(jnp.dot(x_rows[:, lower:upper], w_up[lower:upper], preferred_element_type=jnp.float32))
        grad_hidden = grad_hidden + rounded_term(jnp.dot(dy_rows[:, lower:upper], w_down[:, lower:upper].T, preferred_element_type=jnp.float32))
    hidden_act, grad_gate, grad_up = swiglu_backward(gate_pre, up_pre, grad_hidden)
    down_part = jnp.dot(hidden_act.T, dy_rows, preferred_element_type=jnp.float32).astype(jnp.bfloat16)
    gate_part = jnp.dot(x_rows.T, grad_gate, preferred_element_type=jnp.float32).astype(jnp.bfloat16)
    up_part = jnp.dot(x_rows.T, grad_up, preferred_element_type=jnp.float32).astype(jnp.bfloat16)
    grad_rows = (jnp.dot(grad_gate, w_gate.T, preferred_element_type=jnp.float32)
                 + jnp.dot(grad_up, w_up.T, preferred_element_type=jnp.float32)).astype(jnp.bfloat16)
    return grad_rows, gate_part, up_part, down_part


def reference(tokens, out_grad, expert_ids, gates, gate_weight, up_weight, down_weight):
    block_ids = expert_ids.reshape(N_NODE, TOK_NODE * TOP)
    onehot = (block_ids[:, :, None] == jnp.arange(EXPERTS, dtype=jnp.int32)[None, None, :]).astype(jnp.int32)
    earlier = jnp.cumsum(onehot, axis=1) - onehot
    slot_pos = jnp.sum(earlier * onehot, axis=2)
    kept_mask = slot_pos < CAP
    row_count = N_NODE * CAP
    block_index = jnp.arange(N_NODE, dtype=jnp.int32)[:, None]
    dest_row = jnp.where(kept_mask, block_ids * row_count + block_index * CAP + slot_pos, EXPERTS * row_count)
    dest_row = dest_row.reshape(-1).astype(jnp.int32)
    x_rep = jnp.repeat(tokens, TOP, axis=0)
    dy_rep = (gates.reshape(-1, 1) * jnp.repeat(out_grad, TOP, axis=0).astype(jnp.float32)).astype(jnp.bfloat16)
    blank = jnp.zeros((EXPERTS * row_count, D), jnp.bfloat16)
    x_buf = blank.at[dest_row].set(x_rep, mode="drop").reshape(EXPERTS, row_count, D)
    dy_buf = blank.at[dest_row].set(dy_rep, mode="drop").reshape(EXPERTS, row_count, D)
    grad_rows, gate_grad, up_grad, down_grad = lax.map(expert_step, (x_buf, dy_buf, gate_weight, up_weight, down_weight))
    back_rows = grad_rows.reshape(EXPERTS * row_count, D)
    safe_row = jnp.minimum(dest_row, EXPERTS * row_count - 1)
    picked = jnp.where(kept_mask.reshape(-1, 1), back_rows[safe_row].astype(jnp.float32), jnp.float32(0.0))
    grad_tokens = picked.reshape(TOKENS, TOP, D).sum(axis=1).astype(jnp.bfloat16)
    return grad_tokens, gate_grad, up_grad, down_grad
```

```python
import functools

import jax
import jax.numpy as jnp
from jax import lax
from jax.experimental import pallas as pl
from jax.experimental.pallas import tpu as pltpu
from jax.sharding import PartitionSpec as P

MESH = pl.DeviceIdType.MESH


def swiglu_backward(gate_pre, up_pre, grad_hidden):
    sigmoid_g = jax.nn.sigmoid(gate_pre)
    activated = gate_pre * sigmoid_g
    hidden_act = (activated * up_pre).astype(jnp.bfloat16)
    grad_gate = (grad_hidden * up_pre * sigmoid_g * (1.0 + gate_pre * (1.0 - sigmoid_g))).astype(
        jnp.bfloat16
    )
    grad_up = (grad_hidden * activated).astype(jnp.bfloat16)
    return (hidden_act, grad_gate, grad_up)


def width_sum_kernel(
    n, chunks, ch, hop,
    g_ref, u_ref, h_ref, act_ref, gg_ref, gu_ref,
    part, done, part_send, part_recv, done_send, done_recv,
):
    me = lax.axis_index("local")
    half = chunks * ch
    ins = (g_ref, u_ref, h_ref)
    outs = (act_ref, gg_ref, gu_ref)

    barrier = pltpu.get_barrier_semaphore()

    @pl.when(me > 0)
    def _():
        pl.semaphore_signal(barrier, inc=1, device_id={"local": me - 1}, device_id_type=MESH)

    @pl.when(me < n - 1)
    def _():
        pl.semaphore_signal(barrier, inc=1, device_id={"local": me + 1}, device_id_type=MESH)

    pl.semaphore_wait(barrier, (me > 0).astype(jnp.int32) + (me < n - 1).astype(jnp.int32))

    def part_copy(way, c):
        target = me - 1 if way == 0 else me + 1
        return pltpu.make_async_remote_copy(
            src_ref=part.at[way, c],
            dst_ref=part.at[way, c],
            send_sem=part_send.at[way, c],
            recv_sem=part_recv.at[way, c],
            device_id={"local": target},
            device_id_type=MESH,
        )

    def done_copy(way, c):
        target = me + 1 if way == 0 else me - 1
        return pltpu.make_async_remote_copy(
            src_ref=done.at[way, c],
            dst_ref=done.at[way, c],
            send_sem=done_send.at[way, c],
            recv_sem=done_recv.at[way, c],
            device_id={"local": target},
            device_id_type=MESH,
        )

    def rows_of(way, c):
        return pl.ds(pl.multiple_of(way * half + c * ch, ch), ch)

    def step(s, carry):
        for way in range(2):
            dist = me if way == 0 else n - 1 - me
            c = s - hop * (n - 1 - dist)
            live = jnp.logical_and(c >= 0, c < chunks)

            @pl.when(jnp.logical_and(live, dist == n - 1))
            def _():
                rows = rows_of(way, c)
                for j in range(3):
                    part[way, c, pl.ds(j * ch, ch), :] = ins[j][rows, :]
                part_copy(way, c).start()

            @pl.when(jnp.logical_and(live, jnp.logical_and(dist > 0, dist < n - 1)))
            def _():
                part_copy(way, c).wait_recv()
                rows = rows_of(way, c)
                for j in range(3):
                    at = pl.ds(j * ch, ch)
                    total = part[way, c, at, :].astype(jnp.float32) + ins[j][rows, :].astype(
                        jnp.float32
                    )
                    part[way, c, at, :] = total.astype(jnp.bfloat16)
                part_copy(way, c).start()

            @pl.when(jnp.logical_and(live, dist == 0))
            def _():
                part_copy(way, c).wait_recv()
                rows = rows_of(way, c)
                sums = [
                    part[way, c, pl.ds(j * ch, ch), :].astype(jnp.float32)
                    + ins[j][rows, :].astype(jnp.float32)
                    for j in range(3)
                ]
                for j, value in enumerate(swiglu_backward(*sums)):
                    done[way, c, pl.ds(j * ch, ch), :] = value
                    outs[j][rows, :] = value
                done_copy(way, c).start()

            k = s - hop * (n - 1) - hop * dist
            back = jnp.logical_and(jnp.logical_and(k >= 0, k < chunks), dist > 0)

            @pl.when(back)
            def _():
                done_copy(way, k).wait_recv()

            @pl.when(jnp.logical_and(back, dist < n - 1))
            def _():
                done_copy(way, k).start()

            @pl.when(back)
            def _():
                rows = rows_of(way, k)
                for j in range(3):
                    outs[j][rows, :] = done[way, k, pl.ds(j * ch, ch), :]

        return carry

    lax.fori_loop(0, chunks + 2 * hop * (n - 1), step, 0)

    def drain(c, carry):
        for way in range(2):
            dist = me if way == 0 else n - 1 - me

            @pl.when(dist > 0)
            def _():
                part_copy(way, c).wait_send()

            @pl.when(dist < n - 1)
            def _():
                done_copy(way, c).wait_send()

        return carry

    lax.fori_loop(0, chunks, drain, 0)


def width_sum(gate_pre, up_pre, grad_hidden):
    n = lax.axis_size("local")
    rows, hidden = gate_pre.shape
    half = rows // 2
    ch = 32 if half % 32 == 0 else 16
    chunks = half // ch
    shape = jax.ShapeDtypeStruct((rows, hidden), jnp.bfloat16)
    whole = pl.BlockSpec(memory_space=pltpu.VMEM)
    return pl.pallas_call(
        functools.partial(width_sum_kernel, n, chunks, ch, 2),
        out_shape=(shape, shape, shape),
        in_specs=[whole] * 3,
        out_specs=(whole, whole, whole),
        scratch_shapes=[
            pltpu.VMEM((2, chunks, 3 * ch, hidden), jnp.bfloat16),
            pltpu.VMEM((2, chunks, 3 * ch, hidden), jnp.bfloat16),
            pltpu.SemaphoreType.DMA((2, chunks)),
            pltpu.SemaphoreType.DMA((2, chunks)),
            pltpu.SemaphoreType.DMA((2, chunks)),
            pltpu.SemaphoreType.DMA((2, chunks)),
        ],
        compiler_params=pltpu.CompilerParams(
            collective_id=0, has_side_effects=True, vmem_limit_bytes=48 * 1024 * 1024
        ),
    )(gate_pre, up_pre, grad_hidden)


def on_device(tokens, out_grad, expert_ids, gates, gate_weight, up_weight, down_weight):
    tok_rows, slice_width = tokens.shape
    top_count = expert_ids.shape[1]
    node_count = lax.axis_size("node")
    exp_local = gate_weight.shape[0]
    hidden = gate_weight.shape[2]
    experts = exp_local * node_count
    capacity = tok_rows * top_count * 5 // (experts * 4)
    row_count = node_count * capacity

    routing = jnp.concatenate([expert_ids.astype(jnp.float32), gates], axis=1)
    routing = lax.all_gather(routing, "node")
    tok_all = lax.all_gather(tokens, "node")
    dy_all = lax.all_gather(out_grad, "node")

    ids_all = routing[:, :, :top_count].astype(jnp.int32)
    gates_all = routing[:, :, top_count:]
    mine = lax.axis_index("node") * exp_local + jnp.arange(exp_local, dtype=jnp.int32)
    hit = ids_all[None] == mine[:, None, None, None]
    named = jnp.any(hit, axis=3)
    gate_of = jnp.sum(jnp.where(hit, gates_all[None], 0.0), axis=3)
    before = jnp.arange(tok_rows)[:, None] < jnp.arange(tok_rows)[None, :]
    slot = jnp.einsum(
        "ebt,tu->ebu",
        named.astype(jnp.bfloat16),
        before.astype(jnp.bfloat16),
        preferred_element_type=jnp.float32,
    ).astype(jnp.int32)
    slot = jnp.where(named, slot, capacity)
    chosen = slot[:, :, None, :] == jnp.arange(capacity, dtype=jnp.int32)[None, None, :, None]
    gate_row = jnp.sum(jnp.where(chosen, gate_of[:, :, None, :], 0.0), axis=3)
    pick = chosen.astype(jnp.bfloat16)

    dy_rows = (
        jnp.einsum("ebst,btd->ebsd", pick, dy_all, preferred_element_type=jnp.float32)
        * gate_row[..., None]
    ).astype(jnp.bfloat16)
    x_rows = jnp.einsum(
        "ebst,btd->ebsd", pick, tok_all, preferred_element_type=jnp.float32
    ).astype(jnp.bfloat16)
    x_flat = x_rows.reshape(exp_local, row_count, slice_width)
    dy_flat = dy_rows.reshape(exp_local, row_count, slice_width)

    def partial(spec, rows, weight):
        value = jnp.einsum(spec, rows, weight, preferred_element_type=jnp.float32)
        return value.astype(jnp.bfloat16).reshape(exp_local * row_count, hidden)

    gate_pre = partial("erd,edf->erf", x_flat, gate_weight)
    up_pre = partial("erd,edf->erf", x_flat, up_weight)
    grad_hidden = partial("erd,efd->erf", dy_flat, down_weight)
    hidden_act, grad_gate, grad_up = (
        v.reshape(exp_local, row_count, hidden) for v in width_sum(gate_pre, up_pre, grad_hidden)
    )

    grad_rows = (
        jnp.einsum("erf,edf->erd", grad_gate, gate_weight, preferred_element_type=jnp.float32)
        + jnp.einsum("erf,edf->erd", grad_up, up_weight, preferred_element_type=jnp.float32)
    ).astype(jnp.bfloat16)
    back = jnp.einsum(
        "ebst,ebsd->btd",
        pick,
        grad_rows.reshape(exp_local, node_count, capacity, slice_width),
        preferred_element_type=jnp.float32,
    ).astype(jnp.bfloat16)
    grad_tokens = lax.psum_scatter(back, "node", scatter_dimension=0, tiled=False)

    down_grad = jnp.einsum(
        "erf,erd->efd", hidden_act, dy_flat, preferred_element_type=jnp.float32
    ).astype(jnp.bfloat16)
    gate_grad = jnp.einsum(
        "erd,erf->edf", x_flat, grad_gate, preferred_element_type=jnp.float32
    ).astype(jnp.bfloat16)
    up_grad = jnp.einsum(
        "erd,erf->edf", x_flat, grad_up, preferred_element_type=jnp.float32
    ).astype(jnp.bfloat16)
    return (grad_tokens, gate_grad, up_grad, down_grad)


def solution(mesh):
    return jax.shard_map(
        on_device,
        mesh=mesh,
        in_specs=(
            P("node", "local"),
            P("node", "local"),
            P("node", None),
            P("node", None),
            P("node", "local", None),
            P("node", "local", None),
            P("node", None, "local"),
        ),
        out_specs=(
            P("node", "local"),
            P("node", "local", None),
            P("node", "local", None),
            P("node", None, "local"),
        ),
        check_vma=False,
    )
```

```python
import functools

import jax
import jax.numpy as jnp
from jax import lax
from jax.experimental import pallas as pl
from jax.experimental.pallas import tpu as pltpu
from jax.sharding import PartitionSpec as P

MESH = pl.DeviceIdType.MESH


def swiglu_backward(gate_pre, up_pre, grad_hidden):
    sigmoid_g = jax.nn.sigmoid(gate_pre)
    activated = gate_pre * sigmoid_g
    hidden_act = (activated * up_pre).astype(jnp.bfloat16)
    grad_gate = (grad_hidden * up_pre * sigmoid_g * (1.0 + gate_pre * (1.0 - sigmoid_g))).astype(
        jnp.bfloat16
    )
    grad_up = (grad_hidden * activated).astype(jnp.bfloat16)
    return (hidden_act, grad_gate, grad_up)


def width_sum_kernel(
    n, chunks, ch, hop, block, expert_rows,
    g_ref, u_ref, h_ref, gw_ref, uw_ref, act_ref, gg_ref, gu_ref, row_ref,
    part, done, gw, uw, part_send, part_recv, done_send, done_recv, weight_sem,
):
    me = lax.axis_index("local")
    half = chunks * ch
    ins = (g_ref, u_ref, h_ref)
    outs = (act_ref, gg_ref, gu_ref)

    gw_copy = pltpu.make_async_copy(gw_ref, gw, weight_sem.at[0])
    uw_copy = pltpu.make_async_copy(uw_ref, uw, weight_sem.at[1])
    gw_copy.start()
    uw_copy.start()

    barrier = pltpu.get_barrier_semaphore()

    @pl.when(me > 0)
    def _():
        pl.semaphore_signal(barrier, inc=1, device_id={"local": me - 1}, device_id_type=MESH)

    @pl.when(me < n - 1)
    def _():
        pl.semaphore_signal(barrier, inc=1, device_id={"local": me + 1}, device_id_type=MESH)

    pl.semaphore_wait(barrier, (me > 0).astype(jnp.int32) + (me < n - 1).astype(jnp.int32))

    def part_copy(way, c):
        target = me - 1 if way == 0 else me + 1
        return pltpu.make_async_remote_copy(
            src_ref=part.at[way, c],
            dst_ref=part.at[way, c],
            send_sem=part_send.at[way, c],
            recv_sem=part_recv.at[way, c],
            device_id={"local": target},
            device_id_type=MESH,
        )

    def done_copy(way, c):
        target = me + 1 if way == 0 else me - 1
        return pltpu.make_async_remote_copy(
            src_ref=done.at[way, c],
            dst_ref=done.at[way, c],
            send_sem=done_send.at[way, c],
            recv_sem=done_recv.at[way, c],
            device_id={"local": target},
            device_id_type=MESH,
        )

    def rows_of(way, c):
        return pl.ds(pl.multiple_of(way * half + c * ch, ch), ch)

    def row_block(way, b):
        start = way * half + b * block
        expert = start // expert_rows
        rows = pl.ds(pl.multiple_of(start, block), block)
        dims = (((1,), (1,)), ((), ()))
        width = gw.shape[1]
        tile = 256 if width % 256 == 0 else 128

        def columns(j, carry):
            at = pl.ds(pl.multiple_of(j * tile, tile), tile)
            total = lax.dot_general(
                gg_ref[rows, :], gw[expert, at, :], dims, preferred_element_type=jnp.float32
            ) + lax.dot_general(
                gu_ref[rows, :], uw[expert, at, :], dims, preferred_element_type=jnp.float32
            )
            row_ref[rows, at] = total.astype(jnp.bfloat16)
            return carry

        lax.fori_loop(0, width // tile, columns, 0)

    def step(s, carry):
        for way in range(2):
            dist = me if way == 0 else n - 1 - me
            c = s - hop * (n - 1 - dist)
            live = jnp.logical_and(c >= 0, c < chunks)

            @pl.when(jnp.logical_and(live, dist == n - 1))
            def _():
                rows = rows_of(way, c)
                for j in range(3):
                    part[way, c, pl.ds(j * ch, ch), :] = ins[j][rows, :]
                part_copy(way, c).start()

            @pl.when(jnp.logical_and(live, jnp.logical_and(dist > 0, dist < n - 1)))
            def _():
                part_copy(way, c).wait_recv()
                rows = rows_of(way, c)
                for j in range(3):
                    at = pl.ds(j * ch, ch)
                    total = part[way, c, at, :].astype(jnp.float32) + ins[j][rows, :].astype(
                        jnp.float32
                    )
                    part[way, c, at, :] = total.astype(jnp.bfloat16)
                part_copy(way, c).start()

            @pl.when(jnp.logical_and(live, dist == 0))
            def _():
                part_copy(way, c).wait_recv()
                rows = rows_of(way, c)
                sums = [
                    part[way, c, pl.ds(j * ch, ch), :].astype(jnp.float32)
                    + ins[j][rows, :].astype(jnp.float32)
                    for j in range(3)
                ]
                for j, value in enumerate(swiglu_backward(*sums)):
                    done[way, c, pl.ds(j * ch, ch), :] = value
                    outs[j][rows, :] = value
                done_copy(way, c).start()

            k = s - hop * (n - 1) - hop * dist
            back = jnp.logical_and(jnp.logical_and(k >= 0, k < chunks), dist > 0)

            @pl.when(back)
            def _():
                done_copy(way, k).wait_recv()

            @pl.when(jnp.logical_and(back, dist < n - 1))
            def _():
                done_copy(way, k).start()

            @pl.when(back)
            def _():
                rows = rows_of(way, k)
                for j in range(3):
                    outs[j][rows, :] = done[way, k, pl.ds(j * ch, ch), :]

        for way in range(2):
            dist = me if way == 0 else n - 1 - me
            k = s - hop * (n - 1) - hop * dist
            ready = jnp.logical_and(k >= 0, k < chunks)
            full = (k + 1) * ch % block == 0

            @pl.when(jnp.logical_and(ready, full))
            def _():
                row_block(way, k * ch // block)

        return carry

    lax.fori_loop(0, hop * (n - 1), step, 0)
    gw_copy.wait()
    uw_copy.wait()
    lax.fori_loop(hop * (n - 1), chunks + 2 * hop * (n - 1), step, 0)

    def drain(c, carry):
        for way in range(2):
            dist = me if way == 0 else n - 1 - me

            @pl.when(dist > 0)
            def _():
                part_copy(way, c).wait_send()

            @pl.when(dist < n - 1)
            def _():
                done_copy(way, c).wait_send()

        return carry

    lax.fori_loop(0, chunks, drain, 0)


def width_sum(gate_pre, up_pre, grad_hidden, gate_weight, up_weight):
    n = lax.axis_size("local")
    rows, hidden = gate_pre.shape
    half = rows // 2
    ch = 16
    expert_rows = rows // gate_weight.shape[0]
    block = 128 if half % 128 == 0 and expert_rows % 128 == 0 else ch
    chunks = half // ch
    shape = jax.ShapeDtypeStruct((rows, hidden), jnp.bfloat16)
    whole = pl.BlockSpec(memory_space=pltpu.VMEM)
    return pl.pallas_call(
        functools.partial(width_sum_kernel, n, chunks, ch, 2, block, expert_rows),
        out_shape=(
            shape, shape, shape,
            jax.ShapeDtypeStruct((rows, gate_weight.shape[1]), jnp.bfloat16),
        ),
        in_specs=[whole] * 3 + [pl.BlockSpec(memory_space=pl.ANY)] * 2,
        out_specs=(whole, whole, whole, whole),
        scratch_shapes=[
            pltpu.VMEM((2, chunks, 3 * ch, hidden), jnp.bfloat16),
            pltpu.VMEM((2, chunks, 3 * ch, hidden), jnp.bfloat16),
            pltpu.VMEM(gate_weight.shape, jnp.bfloat16),
            pltpu.VMEM(up_weight.shape, jnp.bfloat16),
            pltpu.SemaphoreType.DMA((2, chunks)),
            pltpu.SemaphoreType.DMA((2, chunks)),
            pltpu.SemaphoreType.DMA((2, chunks)),
            pltpu.SemaphoreType.DMA((2, chunks)),
            pltpu.SemaphoreType.DMA((2,)),
        ],
        compiler_params=pltpu.CompilerParams(
            collective_id=0, has_side_effects=True, vmem_limit_bytes=60 * 1024 * 1024
        ),
    )(gate_pre, up_pre, grad_hidden, gate_weight, up_weight)


def on_device(tokens, out_grad, expert_ids, gates, gate_weight, up_weight, down_weight):
    tok_rows, slice_width = tokens.shape
    top_count = expert_ids.shape[1]
    node_count = lax.axis_size("node")
    exp_local = gate_weight.shape[0]
    hidden = gate_weight.shape[2]
    experts = exp_local * node_count
    capacity = tok_rows * top_count * 5 // (experts * 4)
    row_count = node_count * capacity

    routing = jnp.concatenate([expert_ids.astype(jnp.float32), gates], axis=1)
    routing = lax.all_gather(routing, "node")
    tok_all = lax.all_gather(tokens, "node")
    routing, out_grad = lax.optimization_barrier((routing, out_grad))
    dy_all = lax.all_gather(out_grad, "node")

    ids_all = routing[:, :, :top_count].astype(jnp.int32)
    gates_all = routing[:, :, top_count:]
    mine = lax.axis_index("node") * exp_local + jnp.arange(exp_local, dtype=jnp.int32)
    hit = ids_all[None] == mine[:, None, None, None]
    named = jnp.any(hit, axis=3)
    gate_of = jnp.sum(jnp.where(hit, gates_all[None], 0.0), axis=3)
    before = jnp.arange(tok_rows)[:, None] < jnp.arange(tok_rows)[None, :]
    slot = jnp.einsum(
        "ebt,tu->ebu",
        named.astype(jnp.bfloat16),
        before.astype(jnp.bfloat16),
        preferred_element_type=jnp.float32,
    ).astype(jnp.int32)
    slot = jnp.where(named, slot, capacity)
    chosen = slot[:, :, None, :] == jnp.arange(capacity, dtype=jnp.int32)[None, None, :, None]
    gate_row = jnp.sum(jnp.where(chosen, gate_of[:, :, None, :], 0.0), axis=3)
    pick = chosen.astype(jnp.bfloat16)

    def partial(spec, rows, weight):
        value = jnp.einsum(spec, rows, weight, preferred_element_type=jnp.float32)
        return value.astype(jnp.bfloat16).reshape(exp_local * row_count, hidden)

    x_flat = (
        jnp.einsum("ebst,btd->ebsd", pick, tok_all, preferred_element_type=jnp.float32)
        .astype(jnp.bfloat16)
        .reshape(exp_local, row_count, slice_width)
    )
    gate_pre = partial("erd,edf->erf", x_flat, gate_weight)
    up_pre = partial("erd,edf->erf", x_flat, up_weight)
    gate_pre, up_pre, dy_all = lax.optimization_barrier((gate_pre, up_pre, dy_all))
    dy_flat = (
        (
            jnp.einsum("ebst,btd->ebsd", pick, dy_all, preferred_element_type=jnp.float32)
            * gate_row[..., None]
        )
        .astype(jnp.bfloat16)
        .reshape(exp_local, row_count, slice_width)
    )
    grad_hidden = partial("erd,efd->erf", dy_flat, down_weight)
    hidden_act, grad_gate, grad_up, grad_rows = (
        v.reshape(exp_local, row_count, -1)
        for v in width_sum(gate_pre, up_pre, grad_hidden, gate_weight, up_weight)
    )
    back = jnp.einsum(
        "ebst,ebsd->btd",
        pick,
        grad_rows.reshape(exp_local, node_count, capacity, slice_width),
        preferred_element_type=jnp.float32,
    ).astype(jnp.bfloat16)
    grad_tokens = lax.psum_scatter(back, "node", scatter_dimension=0, tiled=False)

    down_grad = jnp.einsum(
        "erf,erd->efd", hidden_act, dy_flat, preferred_element_type=jnp.float32
    ).astype(jnp.bfloat16)
    gate_grad = jnp.einsum(
        "erd,erf->edf", x_flat, grad_gate, preferred_element_type=jnp.float32
    ).astype(jnp.bfloat16)
    up_grad = jnp.einsum(
        "erd,erf->edf", x_flat, grad_up, preferred_element_type=jnp.float32
    ).astype(jnp.bfloat16)
    return (grad_tokens, gate_grad, up_grad, down_grad)


def solution(mesh):
    return jax.shard_map(
        on_device,
        mesh=mesh,
        in_specs=(
            P("node", "local"),
            P("node", "local"),
            P("node", None),
            P("node", None),
            P("node", "local", None),
            P("node", "local", None),
            P("node", None, "local"),
        ),
        out_specs=(
            P("node", "local"),
            P("node", "local", None),
            P("node", "local", None),
            P("node", None, "local"),
        ),
        check_vma=False,
    )
```

```python
import functools

import jax
import jax.numpy as jnp
from jax import lax
from jax.experimental import pallas as pl
from jax.experimental.pallas import tpu as pltpu
from jax.sharding import PartitionSpec as P

MESH = pl.DeviceIdType.MESH


def swiglu_backward(gate_pre, up_pre, grad_hidden):
    sigmoid_g = jax.nn.sigmoid(gate_pre)
    activated = gate_pre * sigmoid_g
    hidden_act = (activated * up_pre).astype(jnp.bfloat16)
    grad_gate = (grad_hidden * up_pre * sigmoid_g * (1.0 + gate_pre * (1.0 - sigmoid_g))).astype(
        jnp.bfloat16
    )
    grad_up = (grad_hidden * activated).astype(jnp.bfloat16)
    return (hidden_act, grad_gate, grad_up)


def width_sum_kernel(
    n, chunks, ch, hop, block, expert_rows,
    g_ref, u_ref, h_ref, gw_ref, uw_ref, act_ref, gg_ref, gu_ref, row_ref,
    part, done, gw, uw, part_send, part_recv, done_send, done_recv, weight_sem,
):
    me = lax.axis_index("local")
    half = chunks * ch
    ins = (g_ref, u_ref, h_ref)
    outs = (act_ref, gg_ref, gu_ref)

    gw_copy = pltpu.make_async_copy(gw_ref, gw, weight_sem.at[0])
    uw_copy = pltpu.make_async_copy(uw_ref, uw, weight_sem.at[1])
    gw_copy.start()
    uw_copy.start()

    barrier = pltpu.get_barrier_semaphore()

    @pl.when(me > 0)
    def _():
        pl.semaphore_signal(barrier, inc=1, device_id={"local": me - 1}, device_id_type=MESH)

    @pl.when(me < n - 1)
    def _():
        pl.semaphore_signal(barrier, inc=1, device_id={"local": me + 1}, device_id_type=MESH)

    pl.semaphore_wait(barrier, (me > 0).astype(jnp.int32) + (me < n - 1).astype(jnp.int32))

    def part_copy(way, c):
        target = me - 1 if way == 0 else me + 1
        return pltpu.make_async_remote_copy(
            src_ref=part.at[way, c],
            dst_ref=part.at[way, c],
            send_sem=part_send.at[way, c],
            recv_sem=part_recv.at[way, c],
            device_id={"local": target},
            device_id_type=MESH,
        )

    def done_copy(way, c):
        target = me + 1 if way == 0 else me - 1
        return pltpu.make_async_remote_copy(
            src_ref=done.at[way, c],
            dst_ref=done.at[way, c],
            send_sem=done_send.at[way, c],
            recv_sem=done_recv.at[way, c],
            device_id={"local": target},
            device_id_type=MESH,
        )

    def rows_of(way, c):
        return pl.ds(pl.multiple_of(way * half + c * ch, ch), ch)

    def row_block(way, b):
        start = way * half + b * block
        expert = start // expert_rows
        rows = pl.ds(pl.multiple_of(start, block), block)
        dims = (((1,), (1,)), ((), ()))
        width = gw.shape[1]
        tile = 256 if width % 256 == 0 else 128

        def columns(j, carry):
            at = pl.ds(pl.multiple_of(j * tile, tile), tile)
            total = lax.dot_general(
                gg_ref[rows, :], gw[expert, at, :], dims, preferred_element_type=jnp.float32
            ) + lax.dot_general(
                gu_ref[rows, :], uw[expert, at, :], dims, preferred_element_type=jnp.float32
            )
            row_ref[rows, at] = total.astype(jnp.bfloat16)
            return carry

        lax.fori_loop(0, width // tile, columns, 0)

    def step(s, carry):
        for way in range(2):
            dist = me if way == 0 else n - 1 - me
            c = s - hop * (n - 1 - dist)
            live = jnp.logical_and(c >= 0, c < chunks)

            @pl.when(jnp.logical_and(live, dist == n - 1))
            def _():
                rows = rows_of(way, c)
                for j in range(3):
                    part[way, c, pl.ds(j * ch, ch), :] = ins[j][rows, :]
                part_copy(way, c).start()

            @pl.when(jnp.logical_and(live, jnp.logical_and(dist > 0, dist < n - 1)))
            def _():
                part_copy(way, c).wait_recv()
                rows = rows_of(way, c)
                for j in range(3):
                    at = pl.ds(j * ch, ch)
                    total = part[way, c, at, :].astype(jnp.float32) + ins[j][rows, :].astype(
                        jnp.float32
                    )
                    part[way, c, at, :] = total.astype(jnp.bfloat16)
                part_copy(way, c).start()

            @pl.when(jnp.logical_and(live, dist == 0))
            def _():
                part_copy(way, c).wait_recv()
                rows = rows_of(way, c)
                sums = [
                    part[way, c, pl.ds(j * ch, ch), :].astype(jnp.float32)
                    + ins[j][rows, :].astype(jnp.float32)
                    for j in range(3)
                ]
                for j, value in enumerate(swiglu_backward(*sums)):
                    done[way, c, pl.ds(j * ch, ch), :] = value
                    outs[j][rows, :] = value
                done_copy(way, c).start()

            k = s - hop * (n - 1) - hop * dist
            back = jnp.logical_and(jnp.logical_and(k >= 0, k < chunks), dist > 0)

            @pl.when(back)
            def _():
                done_copy(way, k).wait_recv()

            @pl.when(jnp.logical_and(back, dist < n - 1))
            def _():
                done_copy(way, k).start()

            @pl.when(back)
            def _():
                rows = rows_of(way, k)
                for j in range(3):
                    outs[j][rows, :] = done[way, k, pl.ds(j * ch, ch), :]

        for way in range(2):
            dist = me if way == 0 else n - 1 - me
            k = s - hop * (n - 1) - hop * dist
            ready = jnp.logical_and(k >= 0, k < chunks)
            full = (k + 1) * ch % block == 0

            @pl.when(jnp.logical_and(ready, full))
            def _():
                row_block(way, k * ch // block)

        return carry

    lax.fori_loop(0, hop * (n - 1), step, 0)
    gw_copy.wait()
    uw_copy.wait()
    lax.fori_loop(hop * (n - 1), chunks + 2 * hop * (n - 1), step, 0)

    def drain(c, carry):
        for way in range(2):
            dist = me if way == 0 else n - 1 - me

            @pl.when(dist > 0)
            def _():
                part_copy(way, c).wait_send()

            @pl.when(dist < n - 1)
            def _():
                done_copy(way, c).wait_send()

        return carry

    lax.fori_loop(0, chunks, drain, 0)


def width_sum(gate_pre, up_pre, grad_hidden, gate_weight, up_weight):
    n = lax.axis_size("local")
    rows, hidden = gate_pre.shape
    half = rows // 2
    ch = 16
    expert_rows = rows // gate_weight.shape[0]
    block = 128 if half % 128 == 0 and expert_rows % 128 == 0 else ch
    chunks = half // ch
    shape = jax.ShapeDtypeStruct((rows, hidden), jnp.bfloat16)
    whole = pl.BlockSpec(memory_space=pltpu.VMEM)
    return pl.pallas_call(
        functools.partial(width_sum_kernel, n, chunks, ch, 2, block, expert_rows),
        out_shape=(
            shape, shape, shape,
            jax.ShapeDtypeStruct((rows, gate_weight.shape[1]), jnp.bfloat16),
        ),
        in_specs=[whole] * 3 + [pl.BlockSpec(memory_space=pl.ANY)] * 2,
        out_specs=(whole, whole, whole, whole),
        scratch_shapes=[
            pltpu.VMEM((2, chunks, 3 * ch, hidden), jnp.bfloat16),
            pltpu.VMEM((2, chunks, 3 * ch, hidden), jnp.bfloat16),
            pltpu.VMEM(gate_weight.shape, jnp.bfloat16),
            pltpu.VMEM(up_weight.shape, jnp.bfloat16),
            pltpu.SemaphoreType.DMA((2, chunks)),
            pltpu.SemaphoreType.DMA((2, chunks)),
            pltpu.SemaphoreType.DMA((2, chunks)),
            pltpu.SemaphoreType.DMA((2, chunks)),
            pltpu.SemaphoreType.DMA((2,)),
        ],
        compiler_params=pltpu.CompilerParams(
            collective_id=0, has_side_effects=True, vmem_limit_bytes=60 * 1024 * 1024
        ),
    )(gate_pre, up_pre, grad_hidden, gate_weight, up_weight)


def gather_kernel(n, *refs):
    count = 3
    own, full = refs[:count], refs[count : 2 * count]
    send, recv, pass_send, pass_recv, keep = refs[2 * count :]
    me = lax.axis_index("node")
    twin = me + 1 - 2 * lax.rem(me, 2)
    peers = [lax.rem(me + 2 * d, n) for d in range(1, n // 2)]

    barrier = pltpu.get_barrier_semaphore()
    for peer in peers + [twin]:
        pl.semaphore_signal(barrier, inc=1, device_id={"node": peer}, device_id_type=MESH)
    pl.semaphore_wait(barrier, n // 2)

    waits, arrivals, keeps = [], [], []
    for i in range(count):
        for d, peer in enumerate(peers):
            copy = pltpu.make_async_remote_copy(
                src_ref=own[i],
                dst_ref=full[i].at[me],
                send_sem=send.at[i, d],
                recv_sem=recv.at[i, d],
                device_id={"node": peer},
                device_id_type=MESH,
            )
            copy.start()
            arrivals.append((i, d, copy))
        mine = pltpu.make_async_copy(own[i], full[i].at[me], keep.at[i])
        mine.start()
        keeps.append(mine)
        copy = pltpu.make_async_remote_copy(
            src_ref=own[i],
            dst_ref=full[i].at[me],
            send_sem=pass_send.at[i, 0],
            recv_sem=pass_recv.at[i, 0],
            device_id={"node": twin},
            device_id_type=MESH,
        )
        copy.start()
        waits.append(copy)
    for i, d, copy in arrivals:
        copy.wait_recv()
        origin = lax.rem(me + n - 2 * (d + 1), n)
        onward = pltpu.make_async_remote_copy(
            src_ref=full[i].at[origin],
            dst_ref=full[i].at[origin],
            send_sem=pass_send.at[i, d + 1],
            recv_sem=pass_recv.at[i, d + 1],
            device_id={"node": twin},
            device_id_type=MESH,
        )
        onward.start()
        waits.append(onward)
    for _, _, copy in arrivals:
        copy.wait_send()
    for copy in keeps + waits:
        copy.wait()


def gather_nodes(*own):
    n = lax.axis_size("node")
    anywhere = pl.BlockSpec(memory_space=pl.ANY)
    sems = pltpu.SemaphoreType.DMA((len(own), n // 2))
    return pl.pallas_call(
        functools.partial(gather_kernel, n),
        out_shape=tuple(jax.ShapeDtypeStruct((n,) + v.shape, v.dtype) for v in own),
        in_specs=[anywhere] * len(own),
        out_specs=(anywhere,) * len(own),
        scratch_shapes=[sems] * 4 + [pltpu.SemaphoreType.DMA((len(own),))],
        compiler_params=pltpu.CompilerParams(collective_id=1, has_side_effects=True),
    )(*own)


def on_device(tokens, out_grad, expert_ids, gates, gate_weight, up_weight, down_weight):
    tok_rows, slice_width = tokens.shape
    top_count = expert_ids.shape[1]
    node_count = lax.axis_size("node")
    exp_local = gate_weight.shape[0]
    hidden = gate_weight.shape[2]
    experts = exp_local * node_count
    capacity = tok_rows * top_count * 5 // (experts * 4)
    row_count = node_count * capacity

    routing = jnp.concatenate([expert_ids.astype(jnp.float32), gates], axis=1)
    routing = jnp.pad(routing, ((0, 0), (0, 128 - 2 * top_count)))
    routing, tok_all, dy_all = gather_nodes(routing, tokens, out_grad)

    ids_all = routing[:, :, :top_count].astype(jnp.int32)
    gates_all = routing[:, :, top_count : 2 * top_count]
    mine = lax.axis_index("node") * exp_local + jnp.arange(exp_local, dtype=jnp.int32)
    hit = ids_all[None] == mine[:, None, None, None]
    named = jnp.any(hit, axis=3)
    gate_of = jnp.sum(jnp.where(hit, gates_all[None], 0.0), axis=3)
    before = jnp.arange(tok_rows)[:, None] < jnp.arange(tok_rows)[None, :]
    slot = jnp.einsum(
        "ebt,tu->ebu",
        named.astype(jnp.bfloat16),
        before.astype(jnp.bfloat16),
        preferred_element_type=jnp.float32,
    ).astype(jnp.int32)
    slot = jnp.where(named, slot, capacity)
    chosen = slot[:, :, None, :] == jnp.arange(capacity, dtype=jnp.int32)[None, None, :, None]
    gate_row = jnp.sum(jnp.where(chosen, gate_of[:, :, None, :], 0.0), axis=3)
    pick = chosen.astype(jnp.bfloat16)

    def partial(spec, rows, weight):
        value = jnp.einsum(spec, rows, weight, preferred_element_type=jnp.float32)
        return value.astype(jnp.bfloat16).reshape(exp_local * row_count, hidden)

    x_flat = (
        jnp.einsum("ebst,btd->ebsd", pick, tok_all, preferred_element_type=jnp.float32)
        .astype(jnp.bfloat16)
        .reshape(exp_local, row_count, slice_width)
    )
    gate_pre = partial("erd,edf->erf", x_flat, gate_weight)
    up_pre = partial("erd,edf->erf", x_flat, up_weight)
    dy_flat = (
        (
            jnp.einsum("ebst,btd->ebsd", pick, dy_all, preferred_element_type=jnp.float32)
            * gate_row[..., None]
        )
        .astype(jnp.bfloat16)
        .reshape(exp_local, row_count, slice_width)
    )
    grad_hidden = partial("erd,efd->erf", dy_flat, down_weight)
    hidden_act, grad_gate, grad_up, grad_rows = (
        v.reshape(exp_local, row_count, -1)
        for v in width_sum(gate_pre, up_pre, grad_hidden, gate_weight, up_weight)
    )
    back = jnp.einsum(
        "ebst,ebsd->btd",
        pick,
        grad_rows.reshape(exp_local, node_count, capacity, slice_width),
        preferred_element_type=jnp.float32,
    ).astype(jnp.bfloat16)
    grad_tokens = lax.psum_scatter(back, "node", scatter_dimension=0, tiled=False)

    down_grad = jnp.einsum(
        "erf,erd->efd", hidden_act, dy_flat, preferred_element_type=jnp.float32
    ).astype(jnp.bfloat16)
    gate_grad = jnp.einsum(
        "erd,erf->edf", x_flat, grad_gate, preferred_element_type=jnp.float32
    ).astype(jnp.bfloat16)
    up_grad = jnp.einsum(
        "erd,erf->edf", x_flat, grad_up, preferred_element_type=jnp.float32
    ).astype(jnp.bfloat16)
    return (grad_tokens, gate_grad, up_grad, down_grad)


def solution(mesh):
    return jax.shard_map(
        on_device,
        mesh=mesh,
        in_specs=(
            P("node", "local"),
            P("node", "local"),
            P("node", None),
            P("node", None),
            P("node", "local", None),
            P("node", "local", None),
            P("node", None, "local"),
        ),
        out_specs=(
            P("node", "local"),
            P("node", "local", None),
            P("node", "local", None),
            P("node", None, "local"),
        ),
        check_vma=False,
    )
```
